128 devices in a mesh: str: 16 (over z, y), int: 8 (over x, core).
Axes of the slice: x: 4, y: 4, z: 4, core: 2. Of those that a mesh axis runs over, the one named last changes fastest.
Arguments:
- ci: bfloat16 [192, 128, 2, 2048], P('str', None, None, 'int'), may hold values from -6 to 6
- slabs: bfloat16 [2, 2, 2048, 2048], P(None, None, None, 'int')
- sector: int32 [192], P('str'), may hold values from 0 to 1
- dest_dev: int32 [192, 1], P('str'), may hold values from 0 to 15; in each aligned block of 12 rows (0 to 11, 12 to 23, ...) at most 2 rows name the same one
- dest_slot: int32 [192], P('str'), may hold values from 0 to 11
- coef: bfloat16 [192, 2], P('str'), may hold values from -4 to 4
Outputs:
- sigma_vector: bfloat16 [192, 128, 2, 2048], P('str', None, None, 'int')
The draws below stay inside these ranges and needn't reach their ends.
Inputs may be any that keep to these rules, and one draw needn't show every extreme that they name: `dest_dev`: among the 12 blocks of one str device at most 2 name the same value, and exactly 2 do on some device.
All inputs are finite; a program needn't handle non-finite values.
Results may differ from the reference program's by a relative error of at most 0.001.
Values may be sent and summed in bfloat16 or wider, within the bound.
No kernel may reach another device: no remote copies, remote signals or barrier semaphores. Data moves between devices by JAX's collectives and lax.ppermute only.
A program may use at most 192 MiB of HBM per device.

```python
import math
import jax
import jax.numpy as jnp
import numpy as np
from jax import lax

NB = 2048
SECT = 2
CAP = 2
R = 128
BPD = 12
NBLK = 192
N_STR = 16


def draw_slabs(key, part):
    key = jax.random.fold_in(key, 7)
    key_noise, key_level = jax.random.split(key)
    noise = jax.random.normal(key_noise, (SECT, 2, NB, NB), jnp.float32) * NB ** (-0.5)
    level = jnp.exp(jax.random.uniform(key_level, (SECT, 1, NB, 1), jnp.float32, 0.0, math.log(10.0)))
    rows = jnp.arange(NB, dtype=jnp.int32)
    eye = (rows[:, None] == rows[None, :]).astype(jnp.float32)
    real_part = (jnp.arange(2, dtype=jnp.int32) == 0).astype(jnp.float32)
    on_diag = eye[None, None] * level * real_part[None, :, None, None]
    return (noise + on_diag).astype(jnp.bfloat16)


def place_ends(result, key, low, largest):
    extent = result.shape
    place = [jax.random.randint(jax.random.fold_in(key, axis), (), 0, extent[axis]) for axis in range(len(extent))]
    result = result.at[tuple(place)].set(low)
    longest = extent.index(max(extent))
    place[longest] = (place[longest] + 1) % extent[longest]
    return result.at[tuple(place)].set(largest)


def shard_levels(rng, extent, shards, low, top_value):
    level = 1.0
    for axis_at, blocks in shards:
        heights = jax.random.uniform(jax.random.fold_in(jax.random.fold_in(rng, 6), axis_at), (blocks,), jnp.float32, low / len(shards), top_value / len(shards))
        level = level * jnp.repeat(jnp.exp(heights), extent[axis_at] // blocks).reshape((-1,) + (1,) * (len(extent) - 1 - axis_at))
    return level


def shared_out(rng, own, number, rows, amount, top, bound, lean):
    sequence = jax.random.permutation(rng, amount)
    crowded, usual = portions_of(amount, rows * top, bound, lean, True), portions_of(amount, rows * top, bound, lean, False)
    places = jnp.arange(amount)

    def named(tallies, offset_by):
        used = int((tallies > 0).sum())
        fixed = max(1, used // 4)
        shifted = fixed + (places - fixed + offset_by * (used - fixed)) % max(1, amount - fixed)
        return jnp.zeros((amount,), jnp.int32).at[sequence[jnp.where(places < fixed, places, shifted)]].set(jnp.asarray(tallies, jnp.int32))

    tallies = jnp.where(number % 4 == 0, named(crowded, number // 4), named(usual, number - number // 4 - 1))
    mixed = jax.random.permutation(jax.random.fold_in(own, 3), amount)
    giver, receiver = mixed[0:amount // 2 * 2:2], mixed[1:amount // 2 * 2:2]
    margin = jnp.minimum(tallies[giver] - 1, bound - tallies[receiver]) // 2
    margin = jnp.where((giver == sequence[0]) | (receiver == sequence[0]) | (tallies[receiver] == 0), 0, jnp.maximum(margin, 0))
    shifted = jax.random.randint(jax.random.fold_in(own, 4), (amount // 2,), 0, 1 << 20) % (margin + 1)
    tallies = tallies.at[giver].add(-shifted).at[receiver].add(shifted)
    labels = jnp.searchsorted(jnp.cumsum(tallies), jnp.arange(rows * top), side="right").astype(jnp.int32)
    listing = labels.reshape(top, rows).T
    listing = listing[jax.random.permutation(jax.random.fold_in(own, 1), rows)]
    offset_by = jax.random.randint(jax.random.fold_in(own, 2), (rows, 1), 0, top)
    return jnp.take_along_axis(listing, (jnp.arange(top)[None, :] + offset_by) % top, axis=1)


def portions_of(amount, total, bound, slope, full):
    portions = [(1 << 20) // math.isqrt(grade ** slope) + 1 for grade in range(1, amount + 1)]
    largest = bound if full else min(bound, max(-(-total // amount), total * portions[0] // sum(portions)))
    least = 1 if total - largest >= amount - 1 else 0
    counts, spare = [largest] + [least] * (amount - 1), total - largest - least * (amount - 1)
    while spare > 0:
        movable = [i for i in range(1, amount) if counts[i] < largest] or [i for i in range(1, amount) if counts[i] < bound]
        whole, left = sum([portions[i] for i in movable]), spare
        for i in movable:
            extra = min(bound - counts[i], max(1, left * portions[i] // whole), spare)
            counts[i] = counts[i] + extra
            spare = spare - extra
    return np.array(counts)


def normal_values(stream_key, extent, width, bound, shards=(), kind=jnp.bfloat16):
    entries = jax.random.normal(stream_key, extent, jnp.float32) * width
    if len(shards) > 0:
        entries = shard_levels(stream_key, extent, shards, -0.22, 0.18) * entries
    return jnp.clip(entries, min=-bound, max=bound).astype(kind)


def setup_inputs(seed: int = 0) -> dict:
    splits = jax.random.split(jax.random.key(seed), 7)
    ci = normal_values(splits[0], (NBLK, R, 2, NB), 1.0, 6.0, ((0, 16), (3, 8)))
    slabs = draw_slabs(jax.random.fold_in(splits[6], 71), 0)
    sector = place_ends(jax.random.randint(splits[2], (NBLK,), 0, 2), jax.random.fold_in(splits[2], 1), 0, 1).astype(jnp.int32)
    dest_dev_keys = jax.random.split(jax.random.fold_in(splits[3], 1), NBLK // BPD)
    dest_dev_turns = jax.random.permutation(jax.random.fold_in(splits[3], 3), NBLK // BPD)
    dest_dev = jax.vmap(lambda own, number: shared_out(jax.random.fold_in(splits[3], 2), own, number, BPD, N_STR, 1, CAP, 2))(dest_dev_keys, dest_dev_turns).reshape((NBLK, 1))
    dest_slot = place_ends(jax.random.randint(splits[4], (NBLK,), 0, BPD), jax.random.fold_in(splits[4], 1), 0, BPD - 1).astype(jnp.int32)
    coef = normal_values(splits[5], (NBLK, 2), 0.7, 4.0, ((0, 16),))
    return dict(ci=ci, slabs=slabs, sector=sector, dest_dev=dest_dev, dest_slot=dest_slot, coef=coef)


def reference(ci, slabs, sector, dest_dev, dest_slot, coef):
    hi = lax.Precision.HIGHEST
    cf = ci.astype(jnp.float32)
    g = slabs.astype(jnp.float32)
    g_real = g[:, 0]
    g_imag = g[:, 1]
    top = jnp.concatenate([g_real, g_imag], axis=2)
    bottom = jnp.concatenate([-g_imag, g_real], axis=2)
    stacked = jnp.concatenate([top, bottom], axis=1)
    flat = cf.reshape(NBLK * R, 2 * NB)
    prod = jnp.einsum("rk,skn->rsn", flat, stacked, precision=hi)
    prod = prod.reshape(NBLK, R, SECT, 2, NB)
    levels = jnp.arange(SECT, dtype=jnp.int32)
    own_pick = (sector[:, None] == levels[None, :]).astype(jnp.float32)
    other_pick = ((1 - sector)[:, None] == levels[None, :]).astype(jnp.float32)
    diag = jnp.einsum("brsxn,bs->brxn", prod, own_pick, precision=hi)
    other = jnp.einsum("brsxn,bs->brxn", prod, other_pick, precision=hi)
    cwt = coef.astype(jnp.float32)
    c_real = cwt[:, 0][:, None, None]
    c_imag = cwt[:, 1][:, None, None]
    part_real = c_real * other[:, :, 0] - c_imag * other[:, :, 1]
    part_imag = c_real * other[:, :, 1] + c_imag * other[:, :, 0]
    partner = jnp.stack([part_real, part_imag], axis=2)
    target = (dest_dev[:, 0] * BPD + dest_slot).astype(jnp.int32)
    added = jax.ops.segment_sum(partner, target, num_segments=NBLK)
    return (diag + added).astype(jnp.bfloat16)
```

```python
import functools

import jax
import jax.numpy as jnp
from jax import lax
from jax.experimental import pallas as pl
from jax.experimental.pallas import tpu as pltpu
from jax.sharding import PartitionSpec as P

CAP = 2
CHUNKS = (32, 48, 48)
META = 16


def turn(y):
    rows, cols = y.shape
    z = y.reshape(rows // 8, 8, cols)
    even = lax.broadcasted_iota(jnp.int32, z.shape, 1) % 2 == 0
    after = pltpu.roll(z, 7, 1)
    before = pltpu.roll(z, 1, 1)
    return jnp.where(even, -after, before).reshape(rows, cols)


def product_kernel(place, sector, slot, coef, own, far, g_own, g_far, diag, send, acc):
    step = pl.program_id(0)
    nblk, rows, cols = own.shape[1:]
    left = own[0].reshape(nblk * rows, cols)
    right = far[0].reshape(nblk * rows, cols)
    for s in range(2):
        for c in range(2):
            part = jnp.dot(left, g_own[s, c], preferred_element_type=jnp.float32)
            part += jnp.dot(right, g_far[s, c], preferred_element_type=jnp.float32)
            part = part.reshape(nblk, rows, cols)

            @pl.when(step == 0)
            def _():
                acc[s, c] = part

            @pl.when(step > 0)
            def _():
                acc[s, c] += part

    @pl.when(step == pl.num_programs(0) - 1)
    def _():
        half = lax.broadcasted_iota(jnp.int32, (META, cols), 0) // (META // CAP)

        def block(b, carry):
            mine = sector[b]
            diag[b] = acc[mine, 0, b] + turn(acc[mine, 1, b])
            cr = coef[b, 0]
            ci = coef[b, 1]
            p = acc[1 - mine, 0, b]
            q = acc[1 - mine, 1, b]
            partner = (cr * p - ci * q) + turn(cr * q + ci * p)
            top = jnp.max(jnp.abs(partner), axis=0, keepdims=True)
            level = jnp.ceil(jnp.log2(jnp.maximum(top, 1.2e-38)) * 256.0) + 1.0
            level = jnp.clip(level, -32256.0, 32766.0)
            unit = jnp.exp2(level * (1.0 / 256.0))
            code = jnp.round(jnp.clip(partner * (1.0 / unit), -1.0, 1.0) * 32767.0)
            at = slot[b]
            dev = at // CAP
            cap = at % CAP
            first = pl.multiple_of(cap * rows, 16)
            send[dev, pl.ds(first, rows), :] = code.astype(jnp.int32).astype(jnp.int16)
            old = send[dev, pl.ds(CAP * rows, META), :].astype(jnp.int32)
            new = jnp.broadcast_to(level, (META, cols)).astype(jnp.int32)
            send[dev, pl.ds(CAP * rows, META), :] = jnp.where(half == cap, new, old).astype(jnp.int16)
            return carry

        lax.fori_loop(0, nblk, block, 0)


def product(own, far, slabs, place, sector, slot, coef, nstr):
    steps, nblk, rows, cols = own.shape
    grid = pltpu.PrefetchScalarGridSpec(
        num_scalar_prefetch=4,
        grid=(steps,),
        in_specs=[
            pl.BlockSpec((1, nblk, rows, cols), lambda j, *_: (j, 0, 0, 0)),
            pl.BlockSpec((1, nblk, rows, cols), lambda j, *_: (j, 0, 0, 0)),
            pl.BlockSpec((2, 2, cols, cols), lambda j, place, *_: (0, 0, place[j], 0)),
            pl.BlockSpec((2, 2, cols, cols), lambda j, place, *_: (0, 0, place[j + 4], 0)),
        ],
        out_specs=[
            pl.BlockSpec((nblk, rows, cols), lambda j, *_: (0, 0, 0)),
            pl.BlockSpec((nstr, CAP * rows + META, cols), lambda j, *_: (0, 0, 0)),
        ],
        scratch_shapes=[pltpu.VMEM((2, 2, nblk, rows, cols), jnp.float32)],
    )
    flops = 2 * nblk * rows * cols * steps * 2 * 4 * cols
    return pl.pallas_call(
        product_kernel,
        grid_spec=grid,
        out_shape=[
            jax.ShapeDtypeStruct((nblk, rows, cols), jnp.float32),
            jax.ShapeDtypeStruct((nstr, CAP * rows + META, cols), jnp.int16),
        ],
        compiler_params=pltpu.CompilerParams(vmem_limit_bytes=40 * 2**20),
        cost_estimate=pl.CostEstimate(flops=flops, bytes_accessed=12 * 2**20, transcendentals=0),
    )(place, sector, slot, coef, own, far, slabs, slabs)


def add_kernel(where_to, diag, recv, out, acc):
    nblk, rows, cols = diag.shape
    acc[...] = diag[...]

    def take(m, carry):
        b = where_to[m]

        @pl.when(b >= 0)
        def _():
            dev = m // CAP
            cap = m % CAP
            first = pl.multiple_of(cap * rows, 16)
            meta = recv[dev, pl.ds(CAP * rows, META), :].astype(jnp.int32).astype(jnp.float32)
            level = jnp.where(cap == 0, meta[0:1], meta[META // CAP : META // CAP + 1])
            unit = jnp.exp2(level * (1.0 / 256.0))
            code = recv[dev, pl.ds(first, rows), :].astype(jnp.int32).astype(jnp.float32)
            acc[b] += code * (1.0 / 32767.0) * unit

        return carry

    lax.fori_loop(0, where_to.shape[0], take, 0)
    out[...] = acc[...].astype(out.dtype).reshape(out.shape)


def add(diag, recv, where_to):
    nblk, rows, cols = diag.shape
    whole = lambda *_: (0, 0, 0)
    grid = pltpu.PrefetchScalarGridSpec(
        num_scalar_prefetch=1,
        grid=(1,),
        in_specs=[
            pl.BlockSpec(diag.shape, whole),
            pl.BlockSpec(recv.shape, whole),
        ],
        out_specs=pl.BlockSpec((nblk, rows // 2, 2, cols), lambda *_: (0, 0, 0, 0)),
        scratch_shapes=[pltpu.VMEM(diag.shape, jnp.float32)],
    )
    return pl.pallas_call(
        add_kernel,
        grid_spec=grid,
        out_shape=jax.ShapeDtypeStruct((nblk, rows // 2, 2, cols), jnp.bfloat16),
        compiler_params=pltpu.CompilerParams(vmem_limit_bytes=32 * 2**20),
    )(where_to, diag, recv)


def body(ci, slabs, sector, dest_dev, dest_slot, coef):
    nblk, rows, two, ncol = ci.shape
    nstr = lax.axis_size("str")
    nint = lax.axis_size("int")
    nx = nint // 2
    here = lax.axis_index("int")
    x = here // 2
    core = here % 2

    def ipos(a, c):
        return (a % nx) * 2 + c

    def way(c):
        return 1 - 2 * c

    pairs = [(a, c) for a in range(nx) for c in range(2)]
    ahead = [(ipos(a, c), ipos(a + way(c), c)) for a, c in pairs]
    back = [(ipos(a, c), ipos(a - way(c), c)) for a, c in pairs]
    swap = [(ipos(a, c), ipos(a, 1 - c)) for a, c in pairs]

    d = way(core)
    place = jnp.stack(
        [
            ipos(x, core), ipos(x - d, core), ipos(x + d, core), ipos(x + 2, core),
            ipos(x, 1 - core), ipos(x + d, 1 - core), ipos(x - d, 1 - core), ipos(x + 2, 1 - core),
        ]
    ).astype(jnp.int32)

    target = dest_dev[:, 0]
    order = jnp.arange(nblk, dtype=jnp.int32)

    def ranks(t):
        same = (t[..., :, None] == t[..., None, :]) & (order[:, None] > order[None, :])
        return jnp.sum(same.astype(jnp.int32), axis=-1)

    slot = target * CAP + ranks(target)
    table = lax.all_gather(target * 64 + dest_slot, "str", axis=0, tiled=False)
    t_all = table // 64
    r_all = ranks(t_all)
    mine = t_all == lax.axis_index("str")
    caps = jnp.arange(CAP, dtype=jnp.int32)
    hit = mine[:, None, :] & (r_all[:, None, :] == caps[None, :, None])
    where_to = jnp.max(jnp.where(hit, (table % 64)[:, None, :], -1), axis=-1).reshape(nstr * CAP)
    cwt = coef.astype(jnp.float32)

    outs = []
    r0 = 0
    for rc in CHUNKS:
        own = ci[:, r0 : r0 + rc].reshape(nblk, rc * 2, ncol)
        r0 += rc
        one = lax.ppermute(own, "int", ahead)
        two_ = lax.ppermute(own, "int", back)
        three = lax.ppermute(one, "int", ahead)
        near = jnp.stack([own, one, two_, three])
        far = lax.ppermute(near, "int", swap)
        diag, send = product(near, far, slabs, place, sector, slot, cwt, nstr)
        recv = lax.all_to_all(send, "str", split_axis=0, concat_axis=0, tiled=True)
        outs.append(add(diag, recv, where_to))
    return jnp.concatenate(outs, axis=1)


def solution(mesh):
    return jax.shard_map(
        body,
        mesh=mesh,
        in_specs=(
            P("str", None, None, "int"),
            P(None, None, None, "int"),
            P("str"),
            P("str", None),
            P("str"),
            P("str", None),
        ),
        out_specs=P("str", None, None, "int"),
        check_vma=False,
    )
```

```python
import functools

import jax
import jax.numpy as jnp
from jax import lax
from jax.experimental import pallas as pl
from jax.experimental.pallas import tpu as pltpu
from jax.sharding import PartitionSpec as P

CAP = 2
CHUNKS = (32, 48, 48)
META = 16
LIMIT = 16 * 2**20


def turn(y):
    rows, cols = y.shape
    z = y.reshape(rows // 8, 8, cols)
    even = lax.broadcasted_iota(jnp.int32, z.shape, 1) % 2 == 0
    after = pltpu.roll(z, 7, 1)
    before = pltpu.roll(z, 1, 1)
    return jnp.where(even, -after, before).reshape(rows, cols)


def split_kernel(ci, out):
    out[...] = ci[...].reshape(out.shape)


def split(ci, r0, rc):
    nblk, rows, two, cols = ci.shape
    unit = 16
    return pl.pallas_call(
        split_kernel,
        grid=(rc // unit,),
        in_specs=[pl.BlockSpec((nblk, unit, two, cols), lambda i: (0, r0 // unit + i, 0, 0))],
        out_specs=pl.BlockSpec((nblk, two * unit, cols), lambda i: (0, i, 0)),
        out_shape=jax.ShapeDtypeStruct((nblk, two * rc, cols), ci.dtype),
        compiler_params=pltpu.CompilerParams(vmem_limit_bytes=LIMIT),
    )(ci)


def product_kernel(place, sector, slot, inner, coef, *refs):
    pieces, slab = refs[:8], refs[8]
    diag, send, acc, diags, code, sem = refs[9:]
    s, c = pl.program_id(0), pl.program_id(1)
    nblk, rows, cols = diag.shape
    total = None
    for j, piece in enumerate(pieces):
        left = piece[...].reshape(nblk * rows, cols)
        right = slab[0, 0, pl.ds(pl.multiple_of(place[j] * cols, cols), cols), :]
        part = jnp.dot(left, right, preferred_element_type=jnp.float32)
        total = part if total is None else total + part
    acc[s, c] = total.reshape(nblk, rows, cols)

    @pl.when((s == 1) & (c == 1))
    def _():
        finish(sector, slot, inner, coef, acc, diags, code, diag, send, sem)


def finish(sector, slot, inner, coef, acc, diags, code, diag, send, sem):
    nblk, rows, cols = diag.shape
    line = lax.broadcasted_iota(jnp.int32, (META, cols), 0)
    half = line // (META // CAP)
    first_part = (line % (META // CAP)) < META // (2 * CAP)
    for dev in range(send.shape[0]):
        code[dev, CAP * rows :, :] = jnp.zeros((META, cols), jnp.int16)

    def block(b, carry):
        mine = sector[b]
        diags[b] = acc[mine, 0, b] + turn(acc[mine, 1, b])
        pltpu.make_async_copy(diags.at[b], diag.at[b], sem.at[0]).start()
        cr = coef[b, 0]
        ci = coef[b, 1]
        p = acc[1 - mine, 0, b]
        q = acc[1 - mine, 1, b]
        partner = (cr * p - ci * q) + turn(cr * q + ci * p)
        top = jnp.max(jnp.abs(partner), axis=0, keepdims=True)
        level = jnp.ceil(jnp.log2(jnp.maximum(top, 1.2e-38)) * 256.0) + 1.0
        level = jnp.clip(level, -32256.0, 32766.0)
        unit = jnp.exp2(level * (1.0 / 256.0))
        value = jnp.round(jnp.clip(partner * (1.0 / unit), -1.0, 1.0) * 32767.0)
        dev = slot[b] // CAP
        cap = slot[b] % CAP
        first = pl.multiple_of(cap * rows, 16)
        code[dev, pl.ds(first, rows), :] = value.astype(jnp.int32).astype(jnp.int16)
        old = code[dev, pl.ds(CAP * rows, META), :].astype(jnp.int32)
        new = jnp.where(first_part, level.astype(jnp.int32), inner[b] + 1)
        code[dev, pl.ds(CAP * rows, META), :] = jnp.where(half == cap, new, old).astype(jnp.int16)
        return carry

    lax.fori_loop(0, nblk, block, 0)
    copy = pltpu.make_async_copy(code, send, sem.at[1])
    copy.start()
    pltpu.make_async_copy(diags, diag, sem.at[0]).wait()
    copy.wait()


def product(pieces, slabs, place, sector, slot, inner, coef, nstr):
    nblk, rows, cols = pieces[0].shape
    vmem = pl.BlockSpec(memory_space=pltpu.VMEM)
    hbm = pl.BlockSpec(memory_space=pltpu.HBM)
    shape = (nstr, CAP * rows + META, cols)
    grid = pltpu.PrefetchScalarGridSpec(
        num_scalar_prefetch=5,
        grid=(2, 2),
        in_specs=[vmem] * 8 + [pl.BlockSpec((1, 1, slabs.shape[2], cols), lambda s, c, *_: (s, c, 0, 0))],
        out_specs=[hbm, hbm],
        scratch_shapes=[
            pltpu.VMEM((2, 2, nblk, rows, cols), jnp.float32),
            pltpu.VMEM((nblk, rows, cols), jnp.float32),
            pltpu.VMEM(shape, jnp.int16),
            pltpu.SemaphoreType.DMA((2,)),
        ],
    )
    return pl.pallas_call(
        product_kernel,
        grid_spec=grid,
        out_shape=[pltpu.HBM((nblk, rows, cols), jnp.float32), pltpu.HBM(shape, jnp.int16)],
        compiler_params=pltpu.CompilerParams(vmem_limit_bytes=LIMIT),
        cost_estimate=pl.CostEstimate(
            flops=2 * nblk * rows * cols * 8 * 4 * cols, bytes_accessed=14 * 2**20, transcendentals=0
        ),
    )(place, sector, slot, inner, coef, *pieces, slabs)


def add_kernel(r0, diag, recv, *refs):
    out, acc, done, sem = refs[-4:]
    nblk, rows, cols = diag.shape
    load = pltpu.make_async_copy(diag, acc, sem)
    load.start()
    load.wait()
    for dev in range(recv.shape[0]):
        meta = recv[dev, CAP * rows :, :].astype(jnp.int32)
        for cap in range(CAP):
            at = cap * (META // CAP)
            b = meta[at + META // (2 * CAP), 0] - 1

            @pl.when(b >= 0)
            def _():
                unit = jnp.exp2(meta[at : at + 1].astype(jnp.float32) * (1.0 / 256.0)) * (1.0 / 32767.0)
                code = recv[dev, cap * rows : (cap + 1) * rows, :].astype(jnp.int32).astype(jnp.float32)
                acc[b] += code * unit

    done[...] = acc[...].astype(done.dtype).reshape(done.shape)
    copy = pltpu.make_async_copy(done, out.at[:, pl.ds(r0, rows // 2)], sem)
    copy.start()
    copy.wait()


def add(diag, recv, r0, full, out):
    nblk, rows, cols = diag.shape
    rest = [] if out is None else [out]
    vmem = pl.BlockSpec(memory_space=pltpu.VMEM)
    hbm = pl.BlockSpec(memory_space=pltpu.HBM)
    return pl.pallas_call(
        functools.partial(add_kernel, r0),
        in_specs=[hbm, vmem] + [hbm] * len(rest),
        out_specs=hbm,
        scratch_shapes=[
            pltpu.VMEM(diag.shape, jnp.float32),
            pltpu.VMEM((nblk, rows // 2, 2, cols), jnp.bfloat16),
            pltpu.SemaphoreType.DMA,
        ],
        out_shape=pltpu.HBM(full.shape, full.dtype),
        input_output_aliases={2: 0} if rest else {},
        compiler_params=pltpu.CompilerParams(vmem_limit_bytes=LIMIT),
    )(pltpu.with_memory_space_constraint(diag, pltpu.HBM), recv, *rest)


def body(ci, slabs, sector, dest_dev, dest_slot, coef):
    nblk, rows, two, ncol = ci.shape
    nstr = lax.axis_size("str")
    nint = lax.axis_size("int")
    nx = nint // 2
    here = lax.axis_index("int")
    x = here // 2
    core = here % 2

    def ipos(a, c):
        return (a % nx) * 2 + c

    def way(c):
        return 1 - 2 * c

    pairs = [(a, c) for a in range(nx) for c in range(2)]
    ahead = [(ipos(a, c), ipos(a + way(c), c)) for a, c in pairs]
    back = [(ipos(a, c), ipos(a - way(c), c)) for a, c in pairs]
    swap = [(ipos(a, c), ipos(a, 1 - c)) for a, c in pairs]

    d = way(core)
    place = jnp.stack(
        [
            ipos(x, core), ipos(x - d, core), ipos(x + d, core), ipos(x + 2, core),
            ipos(x, 1 - core), ipos(x + d, 1 - core), ipos(x - d, 1 - core), ipos(x + 2, 1 - core),
        ]
    ).astype(jnp.int32)

    target = dest_dev[:, 0]
    order = jnp.arange(nblk, dtype=jnp.int32)
    same = (target[:, None] == target[None, :]) & (order[:, None] > order[None, :])
    slot = target * CAP + jnp.sum(same.astype(jnp.int32), axis=1)
    cwt = coef.astype(jnp.float32)

    def move(v, perm):
        return lax.ppermute(v, "int", perm)

    starts = [sum(CHUNKS[:i]) for i in range(len(CHUNKS))]
    n = len(CHUNKS)
    own = [split(ci, starts[i], CHUNKS[i]) for i in range(n)]
    held = pltpu.with_memory_space_constraint(slabs, pltpu.HBM)
    near, sent, diag = {}, {}, {}

    def direct(i):
        near[i] = [own[i], move(own[i], ahead), move(own[i], back)]

    def tie(*values):
        return list(lax.optimization_barrier(values))

    direct(0)
    for i in range(n):
        x0, p1, p2 = near[i]
        if i > 0:
            p1, p2, sent[i - 1] = tie(p1, p2, sent[i - 1])
        onward = move(p1, ahead)
        first = move(x0, swap)
        if i + 1 < n:
            p1, p2, onward, own[i + 1] = tie(p1, p2, onward, own[i + 1])
            direct(i + 1)
        else:
            p1, p2, onward = tie(p1, p2, onward)
        pieces = [x0, p1, p2, onward, first, move(p1, swap), move(p2, swap), move(onward, swap)]
        diag[i], sent[i] = product(pieces, held, place, sector, slot, dest_slot, cwt, nstr)
    out = None
    full = jax.ShapeDtypeStruct(ci.shape, ci.dtype)
    for i in range(n):
        recv = lax.all_to_all(sent[i], "str", split_axis=0, concat_axis=0, tiled=True)
        out = add(diag[i], recv, starts[i], full, out)
    return out


def solution(mesh):
    return jax.shard_map(
        body,
        mesh=mesh,
        in_specs=(
            P("str", None, None, "int"),
            P(None, None, None, "int"),
            P("str"),
            P("str", None),
            P("str"),
            P("str", None),
        ),
        out_specs=P("str", None, None, "int"),
        check_vma=False,
    )
```

```python
import functools

import jax
import jax.numpy as jnp
from jax import lax
from jax.experimental import pallas as pl
from jax.experimental.pallas import tpu as pltpu
from jax.sharding import PartitionSpec as P

CAP = 2
GROUPS = ((32,), (40,), (56,))
META = 16
LIMIT = 36 * 2**20
STEPS = 32000.0
MAGIC = 12582912.0
TILE = 16


def turn(y):
    rows, cols = y.shape
    z = y.reshape(rows // 8, 8, cols)
    even = lax.broadcasted_iota(jnp.int32, z.shape, 1) % 2 == 0
    after = pltpu.roll(z, 7, 1)
    before = pltpu.roll(z, 1, 1)
    return jnp.where(even, -after, before).reshape(rows, cols)


def split_kernel(r0, ci, out, buf, sem):
    load = pltpu.make_async_copy(ci.at[:, pl.ds(r0, buf.shape[1])], buf, sem)
    load.start()
    load.wait()
    out[...] = buf[...].reshape(out.shape)


def split(ci, r0, rc):
    nblk, rows, two, cols = ci.shape
    return pl.pallas_call(
        functools.partial(split_kernel, r0),
        in_specs=[pl.BlockSpec(memory_space=pltpu.HBM)],
        out_specs=pl.BlockSpec(memory_space=pltpu.VMEM),
        out_shape=jax.ShapeDtypeStruct((nblk, two * rc, cols), ci.dtype),
        scratch_shapes=[pltpu.VMEM((nblk, rc, two, cols), ci.dtype), pltpu.SemaphoreType.DMA],
        compiler_params=pltpu.CompilerParams(vmem_limit_bytes=LIMIT),
    )(ci)


def product_kernel(base, place, sector, slot, inner, coef, *refs):
    pieces, slab = refs[:8], refs[8]
    diag, send, acc, diags, part, codes, meta, sem = refs[-8:]
    s, c = pl.program_id(0), pl.program_id(1)
    nblk, rows, cols = diag.shape
    total = None
    for j, piece in enumerate(pieces):
        left = piece[...].reshape(nblk * rows, cols)
        right = slab[0, 0, pl.ds(pl.multiple_of(place[j] * cols, cols), cols), :]
        dot = jnp.dot(left, right, preferred_element_type=jnp.float32)
        total = dot if total is None else total + dot
    acc[s, c] = total.reshape(nblk, rows, cols)

    @pl.when((s == 1) & (c == 1))
    def _():
        line = lax.broadcasted_iota(jnp.int32, (META, cols), 0)
        half = line // (META // CAP)
        first_part = (line % (META // CAP)) < META // (2 * CAP)
        meta[...] = jnp.zeros(meta.shape, jnp.int16)
        levels = []
        for b in range(nblk):
            mine = sector[b]
            cr = coef[b, 0]
            ci = coef[b, 1]
            top = None
            for r in range(0, rows, TILE):
                span = pl.ds(r, TILE)
                diags[b, span] = acc[mine, 0, b, span] + turn(acc[mine, 1, b, span])
                p = acc[1 - mine, 0, b, span]
                q = acc[1 - mine, 1, b, span]
                value = (cr * p - ci * q) + turn(cr * q + ci * p)
                part[b, span] = value
                size = jnp.max(jnp.abs(value).reshape(TILE // 8, 8, cols), axis=0)
                top = size if top is None else jnp.maximum(top, size)
            top = jnp.max(top, axis=0, keepdims=True)
            level = jnp.ceil(jnp.log2(jnp.maximum(top, 1.2e-38)) * 256.0) + 1.0
            level = jnp.clip(level, -28160.0, 32766.0)
            levels.append(level)
            scale = STEPS / jnp.exp2(level * (1.0 / 256.0))
            for r in range(0, rows, TILE):
                code = (part[b, pl.ds(r, TILE)] * scale + MAGIC) - MAGIC
                row = (b % CAP) * rows + r
                codes[b // CAP, pl.ds(row, TILE), :] = code.astype(jnp.int32).astype(jnp.int16)
        copies = [pltpu.make_async_copy(diags, diag, sem.at[0])]
        copies[0].start()
        for b in range(nblk):
            dev = slot[b] // CAP
            cap = slot[b] % CAP
            first = pl.multiple_of(base + cap * rows, 16)
            pltpu.make_async_copy(
                codes.at[b // CAP, pl.ds((b % CAP) * rows, rows)], send.at[dev, pl.ds(first, rows)], sem.at[1]
            ).start()
        for b in range(nblk):
            dev = slot[b] // CAP
            cap = slot[b] % CAP
            old = meta[dev].astype(jnp.int32)
            new = jnp.where(first_part, levels[b].astype(jnp.int32), inner[b] + 1)
            meta[dev] = jnp.where(half == cap, new, old).astype(jnp.int16)
        last = pltpu.make_async_copy(meta, send.at[:, pl.ds(base + CAP * rows, META)], sem.at[2])
        last.start()
        pltpu.make_async_copy(diags, diag, sem.at[0]).wait()
        pltpu.make_async_copy(codes, send.at[pl.ds(0, nblk // CAP), pl.ds(base, CAP * rows)], sem.at[1]).wait()
        last.wait()


def product(pieces, slabs, place, sector, slot, inner, coef, base, shape, begun):
    nblk, rows, cols = pieces[0].shape
    vmem = pl.BlockSpec(memory_space=pltpu.VMEM)
    hbm = pl.BlockSpec(memory_space=pltpu.HBM)
    nstr = shape[0]
    rest = [] if begun is None else [begun]
    grid = pltpu.PrefetchScalarGridSpec(
        num_scalar_prefetch=5,
        grid=(2, 2),
        in_specs=[vmem] * 8 + [pl.BlockSpec((1, 1, slabs.shape[2], cols), lambda s, c, *_: (s, c, 0, 0))]
        + [hbm] * len(rest),
        out_specs=[hbm, hbm],
        scratch_shapes=[
            pltpu.VMEM((2, 2, nblk, rows, cols), jnp.float32),
            pltpu.VMEM((nblk, rows, cols), jnp.float32),
            pltpu.VMEM((nblk, rows, cols), jnp.float32),
            pltpu.VMEM((nblk // CAP, CAP * rows, cols), jnp.int16),
            pltpu.VMEM((nstr, META, cols), jnp.int16),
            pltpu.SemaphoreType.DMA((3,)),
        ],
    )
    return pl.pallas_call(
        functools.partial(product_kernel, base),
        grid_spec=grid,
        out_shape=[pltpu.HBM((nblk, rows, cols), jnp.float32), pltpu.HBM(shape, jnp.int16)],
        input_output_aliases={14: 1} if rest else {},
        compiler_params=pltpu.CompilerParams(vmem_limit_bytes=LIMIT),
        cost_estimate=pl.CostEstimate(
            flops=10**9, bytes_accessed=10**4, transcendentals=0
        ),
    )(place, sector, slot, inner, coef, *pieces, slabs, *rest)


def add_kernel(places, n, far, *refs):
    diags, recv = refs[:n], refs[n]
    scratch = refs[len(refs) - 3 * n - (3 if far else 1) :]
    out = refs[len(refs) - len(scratch) - 1]
    accs, dones, bufs, sem = scratch[:n], scratch[n : 2 * n], scratch[2 * n : 3 * n], scratch[-1]
    if far:
        codes, arrive = scratch[3 * n : 3 * n + 2]
        fetch = pltpu.make_async_copy(recv, codes, arrive)
        fetch.start()
        recv = codes
    loads = []
    for i in range(n):
        loads.append(pltpu.make_async_copy(diags[i], bufs[i], sem.at[i]))
        loads[i].start()
    stores = []
    base = 0
    for i in range(n):
        acc, done = accs[i], dones[i]
        nblk, rows, cols = diags[i].shape
        acc[...] = jnp.zeros(acc.shape, jnp.float32)
        if far and i == 0:
            fetch.wait()
        found = []
        info = base + CAP * rows
        for dev in range(recv.shape[0]):
            meta = recv[dev, info : info + META, :].astype(jnp.int32)
            for cap in range(CAP):
                at = cap * (META // CAP)
                found.append((dev, cap, meta[at + META // (2 * CAP), 0] - 1))
        for dev, cap, b in found:

            @pl.when(b >= 0)
            def _():
                at = cap * (META // CAP)
                meta = recv[dev, info : info + META, :].astype(jnp.int32)
                unit = jnp.exp2(meta[at : at + 1].astype(jnp.float32) * (1.0 / 256.0)) * (1.0 / STEPS)
                for r in range(0, rows, TILE):
                    line = base + cap * rows + r
                    code = recv[dev, line : line + TILE, :].astype(jnp.int32)
                    acc[b, pl.ds(r, TILE)] += code.astype(jnp.float32) * unit

        base += CAP * rows + META
        loads[i].wait()
        for b in range(nblk):
            done[b] = (acc[b] + bufs[i][b]).astype(done.dtype).reshape(done.shape[1:])
        store = pltpu.make_async_copy(done, out.at[:, pl.ds(places[i], rows // 2)], sem.at[n + i])
        store.start()
        stores.append(store)
    for store in stores:
        store.wait()


def add(diags, recv, places, full, out, far):
    n = len(diags)
    rest = [] if out is None else [out]
    vmem = pl.BlockSpec(memory_space=pltpu.VMEM)
    hbm = pl.BlockSpec(memory_space=pltpu.HBM)
    sums = [pltpu.VMEM(diag.shape, jnp.float32) for diag in diags]
    rounded = [pltpu.VMEM((d.shape[0], d.shape[1] // 2, 2, d.shape[2]), jnp.bfloat16) for d in diags]
    diags = [pltpu.with_memory_space_constraint(diag, pltpu.HBM) for diag in diags]
    codes = []
    if far:
        recv = pltpu.with_memory_space_constraint(recv, pltpu.HBM)
        codes = [pltpu.VMEM(recv.shape, recv.dtype), pltpu.SemaphoreType.DMA]
    return pl.pallas_call(
        functools.partial(add_kernel, places, n, far),
        in_specs=[hbm] * n + [hbm if far else vmem] + [hbm] * len(rest),
        out_specs=hbm,
        scratch_shapes=sums + rounded + sums + codes + [pltpu.SemaphoreType.DMA((2 * n,))],
        out_shape=pltpu.HBM(full.shape, full.dtype),
        input_output_aliases={n + 1: 0} if rest else {},
        compiler_params=pltpu.CompilerParams(vmem_limit_bytes=LIMIT),
    )(*diags, recv, *rest)


def body(ci, slabs, sector, dest_dev, dest_slot, coef):
    nblk, rows, two, ncol = ci.shape
    nstr = lax.axis_size("str")
    nint = lax.axis_size("int")
    nx = nint // 2
    here = lax.axis_index("int")
    x = here // 2
    core = here % 2

    def ipos(a, c):
        return (a % nx) * 2 + c

    def way(c):
        return 1 - 2 * c

    pairs = [(a, c) for a in range(nx) for c in range(2)]
    ahead = [(ipos(a, c), ipos(a + way(c), c)) for a, c in pairs]
    back = [(ipos(a, c), ipos(a - way(c), c)) for a, c in pairs]
    swap = [(ipos(a, c), ipos(a, 1 - c)) for a, c in pairs]

    d = way(core)
    place = jnp.stack(
        [
            ipos(x, core), ipos(x - d, core), ipos(x + d, core), ipos(x + 2, core),
            ipos(x, 1 - core), ipos(x + d, 1 - core), ipos(x - d, 1 - core), ipos(x + 2, 1 - core),
        ]
    ).astype(jnp.int32)

    target = dest_dev[:, 0]
    order = jnp.arange(nblk, dtype=jnp.int32)
    same = (target[:, None] == target[None, :]) & (order[:, None] > order[None, :])
    slot = target * CAP + jnp.sum(same.astype(jnp.int32), axis=1)
    cwt = coef.astype(jnp.float32)

    def move(v, perm):
        return lax.ppermute(v, "int", perm)

    sizes = [rc for group in GROUPS for rc in group]
    starts = [sum(sizes[:i]) for i in range(len(sizes))]
    n = len(sizes)
    raw = pltpu.with_memory_space_constraint(ci, pltpu.HBM)
    own = [split(raw, starts[i], sizes[i]) for i in range(n)]
    held = pltpu.with_memory_space_constraint(slabs, pltpu.HBM)

    def tie(*values):
        return list(lax.optimization_barrier(values))

    near = [[own[0], move(own[0], ahead), move(own[0], back)]]
    sent, diags, previous = [], [], None
    i = 0
    for group in GROUPS:
        shape = (nstr, sum(CAP * 2 * rc + META for rc in group), ncol)
        send, base, here_diags = None, 0, []
        for rc in group:
            x0, p1, p2 = near[i]
            if i > 0:
                p1, x0, _ = tie(p1, x0, previous)
            if i + 1 < n:
                own[i + 1], p1 = tie(own[i + 1], p1)
            onward = move(p1, ahead)
            first = move(x0, swap)
            p1s, p2s = move(p1, swap), move(p2, swap)
            if i + 1 < n:
                nxt, _, _ = tie(own[i + 1], p1, p2)
                near.append([nxt, move(nxt, ahead), move(nxt, back)])
            pieces = [x0, p1, p2, onward, first, p1s, p2s, move(onward, swap)]
            d, send = product(pieces, held, place, sector, slot, dest_slot, cwt, base, shape, send)
            here_diags.append(d)
            previous = d
            base += CAP * 2 * rc + META
            i += 1
        sent.append(send)
        diags.append(here_diags)
    full = jax.ShapeDtypeStruct(ci.shape, ci.dtype)
    out, i = None, 0
    for k, group in enumerate(GROUPS):
        recv = lax.all_to_all(sent[k], "str", split_axis=0, concat_axis=0, tiled=True)
        out = add(diags[k], recv, starts[i : i + len(group)], full, out, k + 1 < len(GROUPS))
        i += len(group)
    return out


def solution(mesh):
    return jax.shard_map(
        body,
        mesh=mesh,
        in_specs=(
            P("str", None, None, "int"),
            P(None, None, None, "int"),
            P("str"),
            P("str", None),
            P("str"),
            P("str", None),
        ),
        out_specs=P("str", None, None, "int"),
        check_vma=False,
    )
```

```python
import functools

import jax
import jax.numpy as jnp
from jax import lax
from jax.experimental import pallas as pl
from jax.experimental.pallas import tpu as pltpu
from jax.sharding import PartitionSpec as P

CAP = 2
GROUPS = ((32,), (40,), (56,))
META = 16
LIMIT = 20 * 2**20
STEPS = 32000.0
MAGIC = 12582912.0
TILE = 16


def turn(y):
    rows, cols = y.shape
    z = y.reshape(rows // 8, 8, cols)
    even = lax.broadcasted_iota(jnp.int32, z.shape, 1) % 2 == 0
    after = pltpu.roll(z, 7, 1)
    before = pltpu.roll(z, 1, 1)
    return jnp.where(even, -after, before).reshape(rows, cols)


def split_kernel(r0, ci, out, buf, sem):
    load = pltpu.make_async_copy(ci.at[:, pl.ds(r0, buf.shape[1])], buf, sem)
    load.start()
    load.wait()
    out[...] = buf[...].reshape(out.shape)


def split(ci, r0, rc):
    nblk, rows, two, cols = ci.shape
    return pl.pallas_call(
        functools.partial(split_kernel, r0),
        in_specs=[pl.BlockSpec(memory_space=pltpu.HBM)],
        out_specs=pl.BlockSpec(memory_space=pltpu.VMEM),
        out_shape=jax.ShapeDtypeStruct((nblk, two * rc, cols), ci.dtype),
        scratch_shapes=[pltpu.VMEM((nblk, rc, two, cols), ci.dtype), pltpu.SemaphoreType.DMA],
        compiler_params=pltpu.CompilerParams(vmem_limit_bytes=LIMIT),
    )(ci)


def product_kernel(base, place, sector, slot, inner, coef, *refs):
    pieces, slab = refs[:8], refs[8]
    diag, send, acc, diags, part, codes, meta, sem = refs[-8:]
    s, c = pl.program_id(0), pl.program_id(1)
    nblk, rows, cols = diag.shape
    total = None
    for j, piece in enumerate(pieces):
        left = piece[...].reshape(nblk * rows, cols)
        right = slab[0, 0, pl.ds(pl.multiple_of(place[j] * cols, cols), cols), :]
        dot = jnp.dot(left, right, preferred_element_type=jnp.float32)
        total = dot if total is None else total + dot
    acc[s, c] = total.reshape(nblk, rows, cols)

    @pl.when((s == 1) & (c == 1))
    def _():
        line = lax.broadcasted_iota(jnp.int32, (META, cols), 0)
        half = line // (META // CAP)
        first_part = (line % (META // CAP)) < META // (2 * CAP)
        meta[...] = jnp.zeros(meta.shape, jnp.int16)
        levels = []
        for b in range(nblk):
            mine = sector[b]
            cr = coef[b, 0]
            ci = coef[b, 1]
            top = None
            for r in range(0, rows, TILE):
                span = pl.ds(r, TILE)
                diags[b, span] = acc[mine, 0, b, span] + turn(acc[mine, 1, b, span])
                p = acc[1 - mine, 0, b, span]
                q = acc[1 - mine, 1, b, span]
                value = (cr * p - ci * q) + turn(cr * q + ci * p)
                part[b, span] = value
                size = jnp.max(jnp.abs(value).reshape(TILE // 8, 8, cols), axis=0)
                top = size if top is None else jnp.maximum(top, size)
            top = jnp.max(top, axis=0, keepdims=True)
            level = jnp.ceil(jnp.log2(jnp.maximum(top, 1.2e-38)) * 256.0) + 1.0
            level = jnp.clip(level, -28160.0, 32766.0)
            levels.append(level)
            scale = STEPS / jnp.exp2(level * (1.0 / 256.0))
            for r in range(0, rows, TILE):
                code = (part[b, pl.ds(r, TILE)] * scale + MAGIC) - MAGIC
                row = (b % CAP) * rows + r
                codes[b // CAP, pl.ds(row, TILE), :] = code.astype(jnp.int32).astype(jnp.int16)
        copies = [pltpu.make_async_copy(diags, diag, sem.at[0])]
        copies[0].start()
        for b in range(nblk):
            dev = slot[b] // CAP
            cap = slot[b] % CAP
            first = pl.multiple_of(base + cap * rows, 16)
            pltpu.make_async_copy(
                codes.at[b // CAP, pl.ds((b % CAP) * rows, rows)], send.at[dev, pl.ds(first, rows)], sem.at[1]
            ).start()
        for b in range(nblk):
            dev = slot[b] // CAP
            cap = slot[b] % CAP
            old = meta[dev].astype(jnp.int32)
            new = jnp.where(first_part, levels[b].astype(jnp.int32), inner[b] + 1)
            meta[dev] = jnp.where(half == cap, new, old).astype(jnp.int16)
        last = pltpu.make_async_copy(meta, send.at[:, pl.ds(base + CAP * rows, META)], sem.at[2])
        last.start()
        pltpu.make_async_copy(diags, diag, sem.at[0]).wait()
        pltpu.make_async_copy(codes, send.at[pl.ds(0, nblk // CAP), pl.ds(base, CAP * rows)], sem.at[1]).wait()
        last.wait()


def product(pieces, slabs, place, sector, slot, inner, coef, base, shape, begun):
    nblk, rows, cols = pieces[0].shape
    vmem = pl.BlockSpec(memory_space=pltpu.VMEM)
    hbm = pl.BlockSpec(memory_space=pltpu.HBM)
    nstr = shape[0]
    rest = [] if begun is None else [begun]
    grid = pltpu.PrefetchScalarGridSpec(
        num_scalar_prefetch=5,
        grid=(2, 2),
        in_specs=[vmem] * 8 + [pl.BlockSpec((1, 1, slabs.shape[2], cols), lambda s, c, *_: (s, c, 0, 0))]
        + [hbm] * len(rest),
        out_specs=[hbm, hbm],
        scratch_shapes=[
            pltpu.VMEM((2, 2, nblk, rows, cols), jnp.float32),
            pltpu.VMEM((nblk, rows, cols), jnp.float32),
            pltpu.VMEM((nblk, rows, cols), jnp.float32),
            pltpu.VMEM((nblk // CAP, CAP * rows, cols), jnp.int16),
            pltpu.VMEM((nstr, META, cols), jnp.int16),
            pltpu.SemaphoreType.DMA((3,)),
        ],
    )
    return pl.pallas_call(
        functools.partial(product_kernel, base),
        grid_spec=grid,
        out_shape=[pltpu.HBM((nblk, rows, cols), jnp.float32), pltpu.HBM(shape, jnp.int16)],
        input_output_aliases={14: 1} if rest else {},
        compiler_params=pltpu.CompilerParams(vmem_limit_bytes=LIMIT),
        cost_estimate=pl.CostEstimate(
            flops=10**9, bytes_accessed=10**4, transcendentals=0
        ),
    )(place, sector, slot, inner, coef, *pieces, slabs, *rest)


def add_kernel(places, n, far, *refs):
    diags, recv = refs[:n], refs[n]
    scratch = refs[len(refs) - 3 * n - (3 if far else 1) :]
    out = refs[len(refs) - len(scratch) - 1]
    accs, dones, bufs, sem = scratch[:n], scratch[n : 2 * n], scratch[2 * n : 3 * n], scratch[-1]
    if far:
        codes, arrive = scratch[3 * n : 3 * n + 2]
        fetch = pltpu.make_async_copy(recv, codes, arrive)
        fetch.start()
        recv = codes
    loads = []
    for i in range(n):
        loads.append(pltpu.make_async_copy(diags[i], bufs[i], sem.at[i]))
        loads[i].start()
    stores = []
    base = 0
    for i in range(n):
        acc, done = accs[i], dones[i]
        nblk, rows, cols = diags[i].shape
        acc[...] = jnp.zeros(acc.shape, jnp.float32)
        if far and i == 0:
            fetch.wait()
        found = []
        info = base + CAP * rows
        for dev in range(recv.shape[0]):
            meta = recv[dev, info : info + META, :].astype(jnp.int32)
            for cap in range(CAP):
                at = cap * (META // CAP)
                found.append((dev, cap, meta[at + META // (2 * CAP), 0] - 1))
        for dev, cap, b in found:

            @pl.when(b >= 0)
            def _():
                at = cap * (META // CAP)
                meta = recv[dev, info : info + META, :].astype(jnp.int32)
                unit = jnp.exp2(meta[at : at + 1].astype(jnp.float32) * (1.0 / 256.0)) * (1.0 / STEPS)
                for r in range(0, rows, TILE):
                    line = base + cap * rows + r
                    code = recv[dev, line : line + TILE, :].astype(jnp.int32)
                    acc[b, pl.ds(r, TILE)] += code.astype(jnp.float32) * unit

        base += CAP * rows + META
        loads[i].wait()
        for b in range(nblk):
            done[b] = (acc[b] + bufs[i][b]).astype(done.dtype).reshape(done.shape[1:])
        store = pltpu.make_async_copy(done, out.at[:, pl.ds(places[i], rows // 2)], sem.at[n + i])
        store.start()
        stores.append(store)
    for store in stores:
        store.wait()


def add(diags, recv, places, full, out, far):
    n = len(diags)
    rest = [] if out is None else [out]
    vmem = pl.BlockSpec(memory_space=pltpu.VMEM)
    hbm = pl.BlockSpec(memory_space=pltpu.HBM)
    sums = [pltpu.VMEM(diag.shape, jnp.float32) for diag in diags]
    rounded = [pltpu.VMEM((d.shape[0], d.shape[1] // 2, 2, d.shape[2]), jnp.bfloat16) for d in diags]
    diags = [pltpu.with_memory_space_constraint(diag, pltpu.HBM) for diag in diags]
    codes = []
    if far:
        recv = pltpu.with_memory_space_constraint(recv, pltpu.HBM)
        codes = [pltpu.VMEM(recv.shape, recv.dtype), pltpu.SemaphoreType.DMA]
    return pl.pallas_call(
        functools.partial(add_kernel, places, n, far),
        in_specs=[hbm] * n + [hbm if far else vmem] + [hbm] * len(rest),
        out_specs=hbm,
        scratch_shapes=sums + rounded + sums + codes + [pltpu.SemaphoreType.DMA((2 * n,))],
        out_shape=pltpu.HBM(full.shape, full.dtype),
        input_output_aliases={n + 1: 0} if rest else {},
        compiler_params=pltpu.CompilerParams(vmem_limit_bytes=LIMIT),
    )(*diags, recv, *rest)


def body(ci, slabs, sector, dest_dev, dest_slot, coef):
    nblk, rows, two, ncol = ci.shape
    nstr = lax.axis_size("str")
    nint = lax.axis_size("int")
    nx = nint // 2
    here = lax.axis_index("int")
    x = here // 2
    core = here % 2

    def ipos(a, c):
        return (a % nx) * 2 + c

    def way(c):
        return 1 - 2 * c

    pairs = [(a, c) for a in range(nx) for c in range(2)]
    ahead = [(ipos(a, c), ipos(a + way(c), c)) for a, c in pairs]
    back = [(ipos(a, c), ipos(a - way(c), c)) for a, c in pairs]
    swap = [(ipos(a, c), ipos(a, 1 - c)) for a, c in pairs]

    d = way(core)
    place = jnp.stack(
        [
            ipos(x, core), ipos(x - d, core), ipos(x + d, core), ipos(x + 2, core),
            ipos(x, 1 - core), ipos(x + d, 1 - core), ipos(x - d, 1 - core), ipos(x + 2, 1 - core),
        ]
    ).astype(jnp.int32)

    target = dest_dev[:, 0]
    order = jnp.arange(nblk, dtype=jnp.int32)
    same = (target[:, None] == target[None, :]) & (order[:, None] > order[None, :])
    slot = target * CAP + jnp.sum(same.astype(jnp.int32), axis=1)
    cwt = coef.astype(jnp.float32)

    def move(v, perm):
        return lax.ppermute(v, "int", perm)

    sizes = [rc for group in GROUPS for rc in group]
    starts = [sum(sizes[:i]) for i in range(len(sizes))]
    n = len(sizes)
    raw = pltpu.with_memory_space_constraint(ci, pltpu.HBM)
    own = [split(raw, starts[i], sizes[i]) for i in range(n)]
    held = pltpu.with_memory_space_constraint(slabs, pltpu.HBM)

    def tie(*values):
        return list(lax.optimization_barrier(values))

    near = [[own[0], move(own[0], ahead), move(own[0], back)]]
    sent, diags, previous = [], [], None
    i = 0
    for group in GROUPS:
        shape = (nstr, sum(CAP * 2 * rc + META for rc in group), ncol)
        send, base, here_diags = None, 0, []
        for rc in group:
            x0, p1, p2 = near[i]
            if i > 0:
                p1, x0, _ = tie(p1, x0, previous)
            if i == 0:
                *own[1:], p1 = tie(*own[1:], p1)
            onward = move(p1, ahead)
            first = move(x0, swap)
            p1s, p2s = move(p1, swap), move(p2, swap)
            if i + 1 < n:
                nxt, _, _ = tie(own[i + 1], p1, p2)
                near.append([nxt, move(nxt, ahead), move(nxt, back)])
            pieces = [x0, p1, p2, onward, first, p1s, p2s, move(onward, swap)]
            d, send = product(pieces, held, place, sector, slot, dest_slot, cwt, base, shape, send)
            here_diags.append(d)
            previous = d
            base += CAP * 2 * rc + META
            i += 1
        sent.append(send)
        diags.append(here_diags)
    full = jax.ShapeDtypeStruct(ci.shape, ci.dtype)
    out, i = None, 0
    for k, group in enumerate(GROUPS):
        recv = lax.all_to_all(sent[k], "str", split_axis=0, concat_axis=0, tiled=True)
        out = add(diags[k], recv, starts[i : i + len(group)], full, out, k + 1 < len(GROUPS))
        i += len(group)
    return out


def solution(mesh):
    return jax.shard_map(
        body,
        mesh=mesh,
        in_specs=(
            P("str", None, None, "int"),
            P(None, None, None, "int"),
            P("str"),
            P("str", None),
            P("str"),
            P("str", None),
        ),
        out_specs=P("str", None, None, "int"),
        check_vma=False,
    )
```

```python
import functools

import jax
import jax.numpy as jnp
from jax import lax
from jax.experimental import pallas as pl
from jax.experimental.pallas import tpu as pltpu
from jax.sharding import PartitionSpec as P

CAP = 2
GROUPS = ((32,), (40,), (56,))
META = 16
LIMIT = 20 * 2**20
STEPS = 32000.0
MAGIC = 12582912.0
TILE = 16


def turn(y):
    rows, cols = y.shape
    z = y.reshape(rows // 8, 8, cols)
    even = lax.broadcasted_iota(jnp.int32, z.shape, 1) % 2 == 0
    after = pltpu.roll(z, 7, 1)
    before = pltpu.roll(z, 1, 1)
    return jnp.where(even, -after, before).reshape(rows, cols)


def split_kernel(r0, ci, out, buf, sem):
    load = pltpu.make_async_copy(ci.at[:, pl.ds(r0, buf.shape[1])], buf, sem)
    load.start()
    load.wait()
    out[...] = buf[...].reshape(out.shape)


def split(ci, r0, rc):
    nblk, rows, two, cols = ci.shape
    return pl.pallas_call(
        functools.partial(split_kernel, r0),
        in_specs=[pl.BlockSpec(memory_space=pltpu.HBM)],
        out_specs=pl.BlockSpec(memory_space=pltpu.VMEM),
        out_shape=jax.ShapeDtypeStruct((nblk, two * rc, cols), ci.dtype),
        scratch_shapes=[pltpu.VMEM((nblk, rc, two, cols), ci.dtype), pltpu.SemaphoreType.DMA],
        compiler_params=pltpu.CompilerParams(vmem_limit_bytes=LIMIT),
    )(ci)


def product_kernel(base, place, sector, slot, inner, coef, *refs):
    pieces, slab = refs[:8], refs[8]
    diag, send, acc, diags, part, codes, meta, sem = refs[-8:]
    s, c = pl.program_id(0), pl.program_id(1)
    nblk, rows, cols = diag.shape
    total = None
    for j, piece in enumerate(pieces):
        left = piece[...].reshape(nblk * rows, cols)
        right = slab[0, 0, pl.ds(pl.multiple_of(place[j] * cols, cols), cols), :]
        dot = jnp.dot(left, right, preferred_element_type=jnp.float32)
        total = dot if total is None else total + dot
    acc[s, c] = total.reshape(nblk, rows, cols)

    @pl.when((s == 1) & (c == 1))
    def _():
        line = lax.broadcasted_iota(jnp.int32, (META, cols), 0)
        half = line // (META // CAP)
        first_part = (line % (META // CAP)) < META // (2 * CAP)
        meta[...] = jnp.zeros(meta.shape, jnp.int16)
        levels = []
        for b in range(nblk):
            mine = sector[b]
            cr = coef[b, 0]
            ci = coef[b, 1]
            top = None
            for r in range(0, rows, TILE):
                span = pl.ds(r, TILE)
                diags[b, span] = acc[mine, 0, b, span] + turn(acc[mine, 1, b, span])
                p = acc[1 - mine, 0, b, span]
                q = acc[1 - mine, 1, b, span]
                value = (cr * p - ci * q) + turn(cr * q + ci * p)
                part[b, span] = value
                size = jnp.max(jnp.abs(value).reshape(TILE // 8, 8, cols), axis=0)
                top = size if top is None else jnp.maximum(top, size)
            top = jnp.max(top, axis=0, keepdims=True)
            level = jnp.ceil(jnp.log2(jnp.maximum(top, 1.2e-38)) * 256.0) + 1.0
            level = jnp.clip(level, -28160.0, 32766.0)
            levels.append(level)
            scale = STEPS / jnp.exp2(level * (1.0 / 256.0))
            for r in range(0, rows, TILE):
                code = (part[b, pl.ds(r, TILE)] * scale + MAGIC) - MAGIC
                row = (b % CAP) * rows + r
                codes[b // CAP, pl.ds(row, TILE), :] = code.astype(jnp.int32).astype(jnp.int16)
        copies = [pltpu.make_async_copy(diags, diag, sem.at[0])]
        copies[0].start()
        for b in range(nblk):
            dev = slot[b] // CAP
            cap = slot[b] % CAP
            first = pl.multiple_of(base + cap * rows, 16)
            pltpu.make_async_copy(
                codes.at[b // CAP, pl.ds((b % CAP) * rows, rows)], send.at[dev, pl.ds(first, rows)], sem.at[1]
            ).start()
        for b in range(nblk):
            dev = slot[b] // CAP
            cap = slot[b] % CAP
            old = meta[dev].astype(jnp.int32)
            new = jnp.where(first_part, levels[b].astype(jnp.int32), inner[b] + 1)
            meta[dev] = jnp.where(half == cap, new, old).astype(jnp.int16)
        last = pltpu.make_async_copy(meta, send.at[:, pl.ds(base + CAP * rows, META)], sem.at[2])
        last.start()
        pltpu.make_async_copy(diags, diag, sem.at[0]).wait()
        pltpu.make_async_copy(codes, send.at[pl.ds(0, nblk // CAP), pl.ds(base, CAP * rows)], sem.at[1]).wait()
        last.wait()


def product(pieces, slabs, place, sector, slot, inner, coef, base, shape, begun):
    nblk, rows, cols = pieces[0].shape
    vmem = pl.BlockSpec(memory_space=pltpu.VMEM)
    hbm = pl.BlockSpec(memory_space=pltpu.HBM)
    nstr = shape[0]
    rest = [] if begun is None else [begun]
    grid = pltpu.PrefetchScalarGridSpec(
        num_scalar_prefetch=5,
        grid=(2, 2),
        in_specs=[vmem] * 8 + [pl.BlockSpec((1, 1, slabs.shape[2], cols), lambda s, c, *_: (s, c, 0, 0))]
        + [hbm] * len(rest),
        out_specs=[hbm, hbm],
        scratch_shapes=[
            pltpu.VMEM((2, 2, nblk, rows, cols), jnp.float32),
            pltpu.VMEM((nblk, rows, cols), jnp.float32),
            pltpu.VMEM((nblk, rows, cols), jnp.float32),
            pltpu.VMEM((nblk // CAP, CAP * rows, cols), jnp.int16),
            pltpu.VMEM((nstr, META, cols), jnp.int16),
            pltpu.SemaphoreType.DMA((3,)),
        ],
    )
    return pl.pallas_call(
        functools.partial(product_kernel, base),
        grid_spec=grid,
        out_shape=[pltpu.HBM((nblk, rows, cols), jnp.float32), pltpu.HBM(shape, jnp.int16)],
        input_output_aliases={14: 1} if rest else {},
        compiler_params=pltpu.CompilerParams(vmem_limit_bytes=LIMIT),
        cost_estimate=pl.CostEstimate(
            flops=10**9, bytes_accessed=10**4, transcendentals=0
        ),
    )(place, sector, slot, inner, coef, *pieces, slabs, *rest)


def add_kernel(places, n, far, *refs):
    diags, recv = refs[:n], refs[n]
    scratch = refs[len(refs) - 3 * n - (3 if far else 1) :]
    out = refs[len(refs) - len(scratch) - 1]
    accs, dones, bufs, sem = scratch[:n], scratch[n : 2 * n], scratch[2 * n : 3 * n], scratch[-1]
    if far:
        codes, arrive = scratch[3 * n : 3 * n + 2]
        fetch = pltpu.make_async_copy(recv, codes, arrive)
        fetch.start()
        recv = codes
    loads = []
    for i in range(n):
        loads.append(pltpu.make_async_copy(diags[i], bufs[i], sem.at[i]))
        loads[i].start()
    stores = []
    base = 0
    for i in range(n):
        acc, done = accs[i], dones[i]
        nblk, rows, cols = diags[i].shape
        acc[...] = jnp.zeros(acc.shape, jnp.float32)
        if far and i == 0:
            fetch.wait()
        found = []
        info = base + CAP * rows
        for dev in range(recv.shape[0]):
            meta = recv[dev, info : info + META, :].astype(jnp.int32)
            for cap in range(CAP):
                at = cap * (META // CAP)
                found.append((dev, cap, meta[at + META // (2 * CAP), 0] - 1))
        for dev, cap, b in found:

            @pl.when(b >= 0)
            def _():
                at = cap * (META // CAP)
                meta = recv[dev, info : info + META, :].astype(jnp.int32)
                unit = jnp.exp2(meta[at : at + 1].astype(jnp.float32) * (1.0 / 256.0)) * (1.0 / STEPS)
                for r in range(0, rows, TILE):
                    line = base + cap * rows + r
                    code = recv[dev, line : line + TILE, :].astype(jnp.int32)
                    acc[b, pl.ds(r, TILE)] += code.astype(jnp.float32) * unit

        base += CAP * rows + META
        loads[i].wait()
        for b in range(nblk):
            done[b] = (acc[b] + bufs[i][b]).astype(done.dtype).reshape(done.shape[1:])
        store = pltpu.make_async_copy(done, out.at[:, pl.ds(places[i], rows // 2)], sem.at[n + i])
        store.start()
        stores.append(store)
    for store in stores:
        store.wait()


def add(diags, recv, places, full, out, far):
    n = len(diags)
    rest = [] if out is None else [out]
    vmem = pl.BlockSpec(memory_space=pltpu.VMEM)
    hbm = pl.BlockSpec(memory_space=pltpu.HBM)
    sums = [pltpu.VMEM(diag.shape, jnp.float32) for diag in diags]
    rounded = [pltpu.VMEM((d.shape[0], d.shape[1] // 2, 2, d.shape[2]), jnp.bfloat16) for d in diags]
    diags = [pltpu.with_memory_space_constraint(diag, pltpu.HBM) for diag in diags]
    codes = []
    if far:
        recv = pltpu.with_memory_space_constraint(recv, pltpu.HBM)
        codes = [pltpu.VMEM(recv.shape, recv.dtype), pltpu.SemaphoreType.DMA]
    return pl.pallas_call(
        functools.partial(add_kernel, places, n, far),
        in_specs=[hbm] * n + [hbm if far else vmem] + [hbm] * len(rest),
        out_specs=hbm,
        scratch_shapes=sums + rounded + sums + codes + [pltpu.SemaphoreType.DMA((2 * n,))],
        out_shape=pltpu.HBM(full.shape, full.dtype),
        input_output_aliases={n + 1: 0} if rest else {},
        compiler_params=pltpu.CompilerParams(vmem_limit_bytes=LIMIT),
    )(*diags, recv, *rest)


def body(ci, slabs, sector, dest_dev, dest_slot, coef):
    nblk, rows, two, ncol = ci.shape
    nstr = lax.axis_size("str")
    nint = lax.axis_size("int")
    nx = nint // 2
    here = lax.axis_index("int")
    x = here // 2
    core = here % 2

    def ipos(a, c):
        return (a % nx) * 2 + c

    def way(c):
        return 1 - 2 * c

    pairs = [(a, c) for a in range(nx) for c in range(2)]
    ahead = [(ipos(a, c), ipos(a + way(c), c)) for a, c in pairs]
    back = [(ipos(a, c), ipos(a - way(c), c)) for a, c in pairs]
    swap = [(ipos(a, c), ipos(a, 1 - c)) for a, c in pairs]

    d = way(core)
    place = jnp.stack(
        [
            ipos(x, core), ipos(x - d, core), ipos(x + d, core), ipos(x + 2, core),
            ipos(x, 1 - core), ipos(x + d, 1 - core), ipos(x - d, 1 - core), ipos(x + 2, 1 - core),
        ]
    ).astype(jnp.int32)

    target = dest_dev[:, 0]
    order = jnp.arange(nblk, dtype=jnp.int32)
    same = (target[:, None] == target[None, :]) & (order[:, None] > order[None, :])
    slot = target * CAP + jnp.sum(same.astype(jnp.int32), axis=1)
    cwt = coef.astype(jnp.float32)

    def move(v, perm):
        return lax.ppermute(v, "int", perm)

    sizes = [rc for group in GROUPS for rc in group]
    starts = [sum(sizes[:i]) for i in range(len(sizes))]
    n = len(sizes)
    raw = pltpu.with_memory_space_constraint(ci, pltpu.HBM)
    own = [split(raw, starts[i], sizes[i]) for i in range(n)]
    held = pltpu.with_memory_space_constraint(slabs, pltpu.HBM)

    def tie(*values):
        return list(lax.optimization_barrier(values))

    near = [[own[0], move(own[0], ahead), move(own[0], back)]]
    sent, diags, previous = [], [], None
    i = 0
    for group in GROUPS:
        shape = (nstr, sum(CAP * 2 * rc + META for rc in group), ncol)
        send, base, here_diags = None, 0, []
        for rc in group:
            x0, p1, p2 = near[i]
            if i > 0:
                p1, x0, _ = tie(p1, x0, previous)
            if i == 0:
                *own[1:], p1 = tie(*own[1:], p1)
            onward = move(p1, ahead)
            own_late, _ = tie(x0, onward)
            first = move(own_late, swap)
            p1s, p2s = move(p1, swap), move(p2, swap)
            if i + 1 < n:
                nxt, _, _ = tie(own[i + 1], p1, p2)
                near.append([nxt, move(nxt, ahead), move(nxt, back)])
            pieces = [x0, p1, p2, onward, first, p1s, p2s, move(onward, swap)]
            d, send = product(pieces, held, place, sector, slot, dest_slot, cwt, base, shape, send)
            here_diags.append(d)
            previous = d
            base += CAP * 2 * rc + META
            i += 1
        sent.append(send)
        diags.append(here_diags)
    full = jax.ShapeDtypeStruct(ci.shape, ci.dtype)
    out, i = None, 0
    for k, group in enumerate(GROUPS):
        recv = lax.all_to_all(sent[k], "str", split_axis=0, concat_axis=0, tiled=True)
        out = add(diags[k], recv, starts[i : i + len(group)], full, out, k + 1 < len(GROUPS))
        i += len(group)
    return out


def solution(mesh):
    return jax.shard_map(
        body,
        mesh=mesh,
        in_specs=(
            P("str", None, None, "int"),
            P(None, None, None, "int"),
            P("str"),
            P("str", None),
            P("str"),
            P("str", None),
        ),
        out_specs=P("str", None, None, "int"),
        check_vma=False,
    )
```
